32 devices in a mesh: row: 4 (over z), col: 8 (over y, x, core).
Axes of the slice: x: 2, y: 2, z: 4, core: 2. Of those that a mesh axis runs over, the one named last changes fastest.
Arguments:
- front_panel: float32 [12288, 1024], P('row', 'col')
- front_trail: float32 [12288, 4096], P('row', 'col'), may hold values from -6 to 6
- child_panel: float32 [2, 4096, 1024], P(None, 'row', 'col'), may hold values from -0.1875 to 0.1875
- child_trail: float32 [2, 4096, 4096], P(None, 'row', 'col'), may hold values from -4 to 4
- child_map: int32 [2, 4096], P(None, 'row'), may hold values from 0 to 3071, as said below
- child_count: int32 [2, 4], P(None, 'row'), may hold values from 256 to 1024, as said below
Outputs:
- factor: float32 [12288, 1024], P('row', 'col')
- schur_block: float32 [12288, 4096], P('row', 'col')
The draws below stay inside these ranges and needn't reach their ends.
Inputs may be any that keep to these rules, and one draw needn't show every extreme that they name: `child_map`: within each slab and each aligned block of 1024 entries the values are distinct rows of one row block. `child_count`: some slab of some row block has all 1024 rows live in every draw.
All inputs are finite; a program needn't handle non-finite values.
Results may differ from the reference program's by a relative error of at most 0.00012.
Values sent between devices are 32-bit elements; how exact they have to be, the bound alone decides.
A program may use at most 192 MiB of HBM per device.

```python
import math
import jax
import jax.numpy as jnp
from jax import lax

F = 12288
PB = 1024
CR = 1024
FR = 3072
TW = 4096
CHILD_ROWS = 4096
N_ROW = 4


def draw_front_panel(key, part):
    key_noise, key_diag = jax.random.split(jax.random.fold_in(key, 11), 2)
    row_index = jnp.arange(F)[:, None]
    col_index = jnp.arange(PB)[None, :]
    noise = jax.random.normal(key_noise, (F, PB), jnp.float32)
    diag_values = jax.random.uniform(key_diag, (F, PB), jnp.float32, 8.0, 12.0)
    in_diag = row_index < PB
    block_values = jnp.where(row_index == col_index, diag_values, noise * (2.0 / math.sqrt(PB)))
    return jnp.where(in_diag, block_values, noise).astype(jnp.float32)


def draw_child_map(key, part):
    all_keys = jax.random.split(jax.random.fold_in(key, 23), 2 * N_ROW)
    picked = jax.vmap(lambda one_key: jax.random.permutation(one_key, FR)[:CR])(all_keys)
    return picked.reshape(2, N_ROW * CR).astype(jnp.int32)


def draw_child_count(key, part):
    key_counts, key_pick = jax.random.split(jax.random.fold_in(key, 37))
    counts = jax.random.randint(key_counts, (2 * N_ROW,), CR // 4, CR + 1)
    chosen = jax.random.randint(key_pick, (), 0, 2 * N_ROW)
    filled = jnp.where(jnp.arange(2 * N_ROW) == chosen, CR, counts)
    return filled.reshape(2, N_ROW).astype(jnp.int32)


def block_levels(key, dims, shards, least, top_value):
    loudness, own = 1.0, jax.random.fold_in(key, 6)
    for axis_at, blocks in shards:
        heights = jnp.exp(jax.random.uniform(jax.random.fold_in(own, axis_at), (blocks,), jnp.float32, least / len(shards), top_value / len(shards)))
        loudness = loudness * jnp.repeat(heights, dims[axis_at] // blocks).reshape([-1 if axis == axis_at else 1 for axis in range(len(dims))])
    return loudness


def centred(rng, shape, deviation, bound, pieces=(), kind=jnp.bfloat16):
    loudness = block_levels(rng, shape, pieces, -0.22, 0.18) if pieces else 1.0
    result = jax.random.normal(rng, shape, jnp.float32) * deviation * loudness
    return jnp.minimum(jnp.maximum(result, -bound), bound).astype(kind)


def setup_inputs(seed: int = 0) -> dict:
    seeds = jax.random.split(jax.random.key(seed), 7)
    front_panel = draw_front_panel(jax.random.fold_in(seeds[6], 71), 0)
    front_trail = centred(seeds[1], (F, TW), 1.0, 6.0, ((0, 4), (1, 8)), jnp.float32)
    child_panel = centred(seeds[2], (2, CHILD_ROWS, PB), PB ** -0.5, 0.1875, ((1, 4), (2, 8)), jnp.float32)
    child_trail = centred(seeds[3], (2, CHILD_ROWS, TW), 0.25, 4.0, ((1, 4), (2, 8)), jnp.float32)
    child_map = draw_child_map(jax.random.fold_in(seeds[6], 71), 0)
    child_count = draw_child_count(jax.random.fold_in(seeds[6], 71), 0)
    return dict(front_panel=front_panel, front_trail=front_trail, child_panel=child_panel, child_trail=child_trail, child_map=child_map, child_count=child_count)


def reference(front_panel, front_trail, child_panel, child_trail, child_map, child_count):
    front_window = jnp.concatenate([front_panel, front_trail], axis=1)
    child_slabs = jnp.concatenate([child_panel, child_trail], axis=2)
    positions = jnp.arange(N_ROW * CR, dtype=jnp.int32)
    source_block = positions // CR
    within = positions - source_block * CR
    for slab_index in range(2):
        if slab_index == 0:
            target_block = source_block
        else:
            target_block = jnp.bitwise_xor(source_block, N_ROW // 2)
        counts = child_count[slab_index][source_block]
        target = jnp.where(within < counts, target_block * FR + child_map[slab_index], F).astype(jnp.int32)
        front_window = front_window.at[target].add(child_slabs[slab_index], mode='drop')
    assembled_panel = front_window[:, :PB]
    assembled_trail = front_window[:, PB:]
    diag_block = assembled_panel[:PB]
    symmetric = 0.5 * (diag_block + diag_block.T)
    lower_factor = jnp.linalg.cholesky(symmetric)
    solved = jax.scipy.linalg.solve_triangular(lower_factor, assembled_panel.T, lower=True).T
    factor = jnp.concatenate([lower_factor, solved[PB:]], axis=0)
    window_factor = factor[PB:PB + TW]
    schur_block = assembled_trail - jnp.dot(factor, window_factor.T, precision=lax.Precision.HIGHEST)
    return (factor, schur_block)
```

```python
import functools

import jax
import jax.numpy as jnp
from jax import lax
from jax.experimental import pallas as pl
from jax.experimental.pallas import tpu as pltpu
from jax.sharding import PartitionSpec as P

HIGHEST = lax.Precision.HIGHEST
TILE = 128
GROUP = 8


def dot_tn(a, b, precision=HIGHEST):
    return lax.dot_general(
        a, b, (((0,), (0,)), ((), ())), precision=precision, preferred_element_type=jnp.float32
    )


def dot_nt(a, b, precision=HIGHEST):
    return lax.dot_general(
        a, b, (((1,), (1,)), ((), ())), precision=precision, preferred_element_type=jnp.float32
    )


def dot_nn(a, b, precision=HIGHEST):
    return jnp.dot(a, b, precision=precision, preferred_element_type=jnp.float32)


def factor_tile(tile):
    row = lax.broadcasted_iota(jnp.int32, (GROUP, TILE), 0)
    lane = lax.broadcasted_iota(jnp.int32, (GROUP, TILE), 1)
    groups = TILE // GROUP
    left = [tile[GROUP * g : GROUP * (g + 1), :] for g in range(groups)]
    right = [jnp.where(lane == row + GROUP * g, 1.0, 0.0) for g in range(groups)]
    for g in range(groups):
        a, x = left[g], right[g]
        cols = [
            jnp.broadcast_to(a[:, GROUP * g + i : GROUP * g + i + 1], (GROUP, TILE))
            for i in range(GROUP)
        ]
        for i in range(GROUP):
            pivot = jnp.broadcast_to(cols[i][i : i + 1, :], (GROUP, TILE))
            scale = lax.rsqrt(pivot)
            column = cols[i] * scale
            below = jnp.where(row > i, column, 0.0)
            a_row = jnp.broadcast_to(a[i : i + 1, :], (GROUP, TILE)) * scale
            x_row = jnp.broadcast_to(x[i : i + 1, :], (GROUP, TILE)) * scale
            a = jnp.where(row == i, a_row, a - below * a_row)
            x = jnp.where(row == i, x_row, x - below * x_row)
            for k in range(i + 1, GROUP):
                cols[k] = cols[k] - below * jnp.broadcast_to(column[k : k + 1, :], (GROUP, TILE))
        a = jnp.where(lane >= row + GROUP * g, a, 0.0)
        left[g], right[g] = a, x
        if g + 1 < groups:
            change = dot_tn(a, jnp.concatenate([a, x], axis=1))
            for h in range(g + 1, groups):
                part = change[GROUP * h : GROUP * (h + 1), :]
                left[h] = left[h] - part[:, :TILE]
                right[h] = right[h] - part[:, TILE:]
    return jnp.concatenate(left, axis=0), jnp.concatenate(right, axis=0)


def cholesky_kernel(diag_ref, upper_ref, inverse_ref):
    size = diag_ref.shape[0]
    count = size // TILE
    for i in range(count):
        for j in range(i, count):
            here = diag_ref[TILE * i : TILE * (i + 1), TILE * j : TILE * (j + 1)]
            there = diag_ref[TILE * j : TILE * (j + 1), TILE * i : TILE * (i + 1)]
            inverse_ref[TILE * i : TILE * (i + 1), TILE * j : TILE * (j + 1)] = 0.5 * (
                here + there.T
            )
        if i:
            inverse_ref[TILE * i : TILE * (i + 1), : TILE * i] = jnp.zeros(
                (TILE, TILE * i), jnp.float32
            )
    block = lax.broadcasted_iota(jnp.int32, (TILE, size), 1) // TILE

    def step(b, carry):
        at = pl.multiple_of(b * TILE, TILE)
        rows, cols = pl.ds(at, TILE), pl.ds(at, TILE)
        top, inv = factor_tile(inverse_ref[rows, cols])
        scaled = dot_nn(inv, inverse_ref[rows, :])
        upper_ref[rows, :] = jnp.where(block > b, scaled, 0.0)
        upper_ref[rows, cols] = top
        inverse_ref[rows, :] = scaled
        inverse_ref[rows, cols] = inv

        def below(s, inner):
            under = pl.ds(pl.multiple_of(s * TILE, TILE), TILE)
            change = dot_tn(upper_ref[rows, under], inverse_ref[rows, :])
            inverse_ref[under, :] = jnp.where(block == b, 0.0, inverse_ref[under, :]) - change
            return inner

        lax.fori_loop(b + 1, count, below, 0)
        inverse_ref[rows, :] = jnp.where(block <= b, inverse_ref[rows, :], 0.0)
        return carry

    lax.fori_loop(0, count, step, 0)


def cholesky(diag):
    size = diag.shape[0]
    shape = jax.ShapeDtypeStruct((size, size), jnp.float32)
    return pl.pallas_call(
        cholesky_kernel,
        out_shape=(shape, shape),
        in_specs=[pl.BlockSpec(memory_space=pltpu.VMEM)],
        out_specs=(pl.BlockSpec(memory_space=pltpu.VMEM),) * 2,
        compiler_params=pltpu.CompilerParams(vmem_limit_bytes=40 << 20),
        cost_estimate=pl.CostEstimate(
            flops=60_000_000_000, bytes_accessed=12 * size * size, transcendentals=0
        ),
        name="cholesky_and_inverse",
    )(diag)


def halves(value):
    high = value.astype(jnp.bfloat16)
    return high, (value - high.astype(jnp.float32)).astype(jnp.bfloat16)


def update_kernel(
    top_tiles, root_ref, panel_ref, right_ref, trail_ref, window_ref, lower_ref,
    factor_ref, schur_ref, high_ref, low_ref,
):
    step = pl.program_id(0)
    width = trail_ref.shape[1]

    @pl.when(step == 0)
    def _():
        high, low = halves(right_ref[...])
        high_ref[...] = high
        low_ref[...] = low

    in_top = jnp.logical_and(root_ref[0] == 1, step < top_tiles)

    @pl.when(in_top)
    def _():
        factor_ref[...] = lower_ref[...]
        schur_ref[...] = trail_ref[...] - window_ref[...]

    @pl.when(jnp.logical_not(in_top))
    def _():
        high, low = halves(panel_ref[...])
        product = (
            dot_nn(high, low_ref[...], None) + dot_nn(low, high_ref[...], None)
        ) + dot_nn(high, high_ref[...], None)
        factor_ref[...] = product[:, width:]
        schur_ref[...] = trail_ref[...] - product[:, :width]


def update(root, panel, right, trail, window, lower):
    rows, depth = panel.shape
    width, narrow = trail.shape[1], lower.shape[1]
    size = 512
    top_tiles = depth // size

    def capped(i, root):
        return jnp.minimum(i, top_tiles - 1), 0

    return pl.pallas_call(
        functools.partial(update_kernel, top_tiles),
        grid_spec=pltpu.PrefetchScalarGridSpec(
            num_scalar_prefetch=1,
            grid=(rows // size,),
            in_specs=[
                pl.BlockSpec((size, depth), lambda i, root: (i, 0)),
                pl.BlockSpec((depth, width + narrow), lambda i, root: (0, 0)),
                pl.BlockSpec((size, width), lambda i, root: (i, 0)),
                pl.BlockSpec((size, width), capped),
                pl.BlockSpec((size, narrow), capped),
            ],
            out_specs=(
                pl.BlockSpec((size, narrow), lambda i, root: (i, 0)),
                pl.BlockSpec((size, width), lambda i, root: (i, 0)),
            ),
            scratch_shapes=[pltpu.VMEM((depth, width + narrow), jnp.bfloat16)] * 2,
        ),
        out_shape=(
            jax.ShapeDtypeStruct((rows, narrow), jnp.float32),
            jax.ShapeDtypeStruct((rows, width), jnp.float32),
        ),
        compiler_params=pltpu.CompilerParams(vmem_limit_bytes=48 << 20),
        name="factor_and_schur",
    )(root, panel, right, trail, window, lower)


def swapped(block, axis, distance):
    count = lax.axis_size(axis)
    route = []
    for low in range(count):
        high = low | 1 << distance
        if high != low and high < count:
            route += [(low, high), (high, low)]
    return lax.ppermute(block, axis, route)


def on_device(front_panel, front_trail, child_panel, child_trail, child_map, child_count):
    block_rows, panel_cols = front_panel.shape
    trail_cols = front_trail.shape[1]
    slab_rows = child_map.shape[1]
    panel_width = panel_cols * lax.axis_size("col")
    top_bit = lax.axis_size("row").bit_length() - 2
    row_id = lax.axis_index("row")
    col_id = lax.axis_index("col")
    live_rows = jnp.arange(slab_rows, dtype=jnp.int32)[None, :] < child_count
    targets = jnp.where(live_rows, child_map, block_rows)

    own_panel = front_panel.at[targets[0]].add(child_panel[0], mode="drop")
    partner_top = jnp.zeros((panel_width, panel_cols), jnp.float32).at[targets[1]].add(
        child_panel[1], mode="drop"
    )
    share = jnp.where(
        row_id == 0,
        own_panel[:panel_width],
        jnp.where(row_id == 1 << top_bit, partner_top, 0.0),
    )
    diag_piece = lax.psum(share, "row")
    diag_full = lax.all_gather(diag_piece, "col", axis=1, tiled=True)

    partner_targets = swapped(targets[1], "row", top_bit)
    panel_slab = swapped(child_panel[1], "row", top_bit)
    trail_slab = swapped(child_trail[1], "row", top_bit)
    panel = own_panel.at[partner_targets].add(panel_slab, mode="drop")
    panel_full = lax.all_gather(panel, "col", axis=1, tiled=True)
    trail = front_trail.at[targets[0]].add(child_trail[0], mode="drop")
    trail = trail.at[partner_targets].add(trail_slab, mode="drop")

    window_start = panel_width + col_id * trail_cols
    window_root = window_start // block_rows
    window_rows = lax.dynamic_slice_in_dim(
        panel_full, window_start - window_root * block_rows, trail_cols, 0
    )
    window_rows, _ = lax.optimization_barrier((window_rows, diag_piece))
    window = lax.psum(jnp.where(row_id == window_root, window_rows, 0.0), "row")

    upper, inverse = cholesky(diag_full)
    first = dot_nt(inverse, window)
    second = dot_tn(inverse, first)
    own_inverse = lax.dynamic_slice_in_dim(inverse, col_id * panel_cols, panel_cols, 0)
    own_upper = lax.dynamic_slice_in_dim(upper, col_id * panel_cols, panel_cols, 0)
    right = jnp.concatenate([second, own_inverse.T], axis=1)
    root = (row_id == 0).astype(jnp.int32)[None]
    return update(root, panel_full, right, trail, window.T, own_upper.T)


def solution(mesh):
    in_specs = (
        P("row", "col"),
        P("row", "col"),
        P(None, "row", "col"),
        P(None, "row", "col"),
        P(None, "row"),
        P(None, "row"),
    )
    out_specs = (P("row", "col"), P("row", "col"))
    return jax.shard_map(
        on_device, mesh=mesh, in_specs=in_specs, out_specs=out_specs, check_vma=False
    )
```

```python
import functools

import jax
import jax.numpy as jnp
from jax import lax
from jax.experimental import pallas as pl
from jax.experimental.pallas import tpu as pltpu
from jax.sharding import PartitionSpec as P

HIGHEST = lax.Precision.HIGHEST
TILE = 128
GROUP = 8


def dot_tn(a, b, precision=HIGHEST):
    return lax.dot_general(
        a, b, (((0,), (0,)), ((), ())), precision=precision, preferred_element_type=jnp.float32
    )


def dot_nt(a, b, precision=HIGHEST):
    return lax.dot_general(
        a, b, (((1,), (1,)), ((), ())), precision=precision, preferred_element_type=jnp.float32
    )


def dot_nn(a, b, precision=HIGHEST):
    return jnp.dot(a, b, precision=precision, preferred_element_type=jnp.float32)


def factor_tile(tile):
    row = lax.broadcasted_iota(jnp.int32, (GROUP, TILE), 0)
    lane = lax.broadcasted_iota(jnp.int32, (GROUP, TILE), 1)
    groups = TILE // GROUP
    left = [tile[GROUP * g : GROUP * (g + 1), :] for g in range(groups)]
    right = [jnp.where(lane == row + GROUP * g, 1.0, 0.0) for g in range(groups)]
    for g in range(groups):
        a, x = left[g], right[g]
        cols = [
            jnp.broadcast_to(a[:, GROUP * g + i : GROUP * g + i + 1], (GROUP, TILE))
            for i in range(GROUP)
        ]
        for i in range(GROUP):
            pivot = jnp.broadcast_to(cols[i][i : i + 1, :], (GROUP, TILE))
            scale = lax.rsqrt(pivot)
            column = cols[i] * scale
            below = jnp.where(row > i, column, 0.0)
            a_row = jnp.broadcast_to(a[i : i + 1, :], (GROUP, TILE)) * scale
            x_row = jnp.broadcast_to(x[i : i + 1, :], (GROUP, TILE)) * scale
            a = jnp.where(row == i, a_row, a - below * a_row)
            x = jnp.where(row == i, x_row, x - below * x_row)
            for k in range(i + 1, GROUP):
                cols[k] = cols[k] - below * jnp.broadcast_to(column[k : k + 1, :], (GROUP, TILE))
        a = jnp.where(lane >= row + GROUP * g, a, 0.0)
        left[g], right[g] = a, x
        if g + 1 < groups:
            change = dot_tn(a, jnp.concatenate([a, x], axis=1))
            for h in range(g + 1, groups):
                part = change[GROUP * h : GROUP * (h + 1), :]
                left[h] = left[h] - part[:, :TILE]
                right[h] = right[h] - part[:, TILE:]
    return jnp.concatenate(left, axis=0), jnp.concatenate(right, axis=0)


def cholesky_kernel(diag_ref, upper_ref, inverse_ref):
    pieces, size, narrow = diag_ref.shape
    count = size // TILE
    per = TILE // narrow

    def tile(i, j):
        rows = slice(TILE * i, TILE * (i + 1))
        parts = [diag_ref[piece, rows, :] for piece in range(per * j, per * (j + 1))]
        return parts[0] if per == 1 else jnp.concatenate(parts, axis=1)

    for i in range(count):
        for j in range(i, count):
            inverse_ref[TILE * i : TILE * (i + 1), TILE * j : TILE * (j + 1)] = 0.5 * (
                tile(i, j) + tile(j, i).T
            )
        if i:
            inverse_ref[TILE * i : TILE * (i + 1), : TILE * i] = jnp.zeros(
                (TILE, TILE * i), jnp.float32
            )
    block = lax.broadcasted_iota(jnp.int32, (TILE, size), 1) // TILE

    def step(b, carry):
        at = pl.multiple_of(b * TILE, TILE)
        rows, cols = pl.ds(at, TILE), pl.ds(at, TILE)
        top, inv = factor_tile(inverse_ref[rows, cols])
        scaled = dot_nn(inv, inverse_ref[rows, :])
        upper_ref[rows, :] = jnp.where(block > b, scaled, 0.0)
        upper_ref[rows, cols] = top
        inverse_ref[rows, :] = scaled
        inverse_ref[rows, cols] = inv

        def below(s, inner):
            under = pl.ds(pl.multiple_of(s * TILE, TILE), TILE)
            change = dot_tn(upper_ref[rows, under], inverse_ref[rows, :])
            inverse_ref[under, :] = jnp.where(block == b, 0.0, inverse_ref[under, :]) - change
            return inner

        lax.fori_loop(b + 1, count, below, 0)
        inverse_ref[rows, :] = jnp.where(block <= b, inverse_ref[rows, :], 0.0)
        return carry

    lax.fori_loop(0, count, step, 0)


def cholesky(diag):
    size = diag.shape[1]
    shape = jax.ShapeDtypeStruct((size, size), jnp.float32)
    return pl.pallas_call(
        cholesky_kernel,
        out_shape=(shape, shape),
        in_specs=[pl.BlockSpec(memory_space=pltpu.VMEM)],
        out_specs=(pl.BlockSpec(memory_space=pltpu.VMEM),) * 2,
        compiler_params=pltpu.CompilerParams(vmem_limit_bytes=40 << 20),
        cost_estimate=pl.CostEstimate(
            flops=60_000_000_000, bytes_accessed=12 * size * size, transcendentals=0
        ),
        name="cholesky_and_inverse",
    )(diag)


def halves(value):
    high = value.astype(jnp.bfloat16)
    return high, (value - high.astype(jnp.float32)).astype(jnp.bfloat16)


def dot_split(dims, left, right):
    def dot(x, y):
        return lax.dot_general(x, y, (dims, ((), ())), preferred_element_type=jnp.float32)

    return (dot(left[0], right[1]) + dot(left[1], right[0])) + dot(left[0], right[0])


def joined(ref):
    return jnp.concatenate([ref[piece] for piece in range(ref.shape[0])], axis=1)


def update_kernel(
    top_tiles, place_ref, panel_ref, inverse_ref, window_ref, upper_ref, trail_ref,
    factor_ref, schur_ref, high_ref, low_ref, flipped_ref, first_ref,
):
    step = pl.program_id(0)
    depth = inverse_ref.shape[0]
    size, width = trail_ref.shape
    narrow = upper_ref.shape[0]
    at_root = place_ref[0] == 1
    part = 256

    @pl.when(step == 0)
    def _():
        window = joined(window_ref)
        window_halves = halves(window)
        for i in range(0, depth, part):
            end = i + part
            first_ref[i:end, :] = dot_split(
                ((1,), (1,)),
                halves(inverse_ref[i:end, :end]),
                tuple(half[:, :end] for half in window_halves),
            )
        for i in range(0, depth, part):
            second = dot_split(
                ((0,), (0,)), halves(inverse_ref[i:, i : i + part]), halves(first_ref[i:, :])
            )
            high_ref[i : i + part, :width], low_ref[i : i + part, :width] = halves(second)
        own = pl.ds(pl.multiple_of(place_ref[1] * narrow, narrow), narrow)
        high_ref[:, width:], low_ref[:, width:] = halves(inverse_ref[own, :].T)

        @pl.when(at_root)
        def _():
            flipped_ref[...] = window.T

    in_top = jnp.logical_and(at_root, step < top_tiles)

    @pl.when(in_top)
    def _():
        rows = pl.ds(pl.multiple_of(step * size, size), size)
        factor_ref[...] = upper_ref[:, rows].T
        schur_ref[...] = trail_ref[...] - flipped_ref[rows, :]

    @pl.when(jnp.logical_not(in_top))
    def _():
        product = dot_split(
            ((1,), (0,)), halves(joined(panel_ref)), (high_ref[...], low_ref[...])
        )
        factor_ref[...] = product[:, width:]
        schur_ref[...] = trail_ref[...] - product[:, :width]


def update(place, panel, inverse, window, upper, trail):
    pieces, rows, narrow = panel.shape
    depth = inverse.shape[0]
    width = trail.shape[1]
    size = 512
    return pl.pallas_call(
        functools.partial(update_kernel, depth // size),
        grid_spec=pltpu.PrefetchScalarGridSpec(
            num_scalar_prefetch=1,
            grid=(rows // size,),
            in_specs=[
                pl.BlockSpec((pieces, size, narrow), lambda i, place: (0, i, 0)),
                pl.BlockSpec((depth, depth), lambda i, place: (0, 0)),
                pl.BlockSpec((pieces, width, narrow), lambda i, place: (0, 0, 0)),
                pl.BlockSpec((narrow, depth), lambda i, place: (place[1], 0)),
                pl.BlockSpec((size, width), lambda i, place: (i, 0)),
            ],
            out_specs=(
                pl.BlockSpec((size, narrow), lambda i, place: (i, 0)),
                pl.BlockSpec((size, width), lambda i, place: (i, 0)),
            ),
            scratch_shapes=[pltpu.VMEM((depth, width + narrow), jnp.bfloat16)] * 2
            + [pltpu.VMEM((depth, width), jnp.float32)] * 2,
        ),
        out_shape=(
            jax.ShapeDtypeStruct((rows, narrow), jnp.float32),
            jax.ShapeDtypeStruct((rows, width), jnp.float32),
        ),
        compiler_params=pltpu.CompilerParams(vmem_limit_bytes=56 << 20),
        name="factor_and_schur",
    )(place, panel, inverse, window, upper, trail)


def swapped(block, axis, distance):
    count = lax.axis_size(axis)
    route = []
    for low in range(count):
        high = low | 1 << distance
        if high != low and high < count:
            route += [(low, high), (high, low)]
    return lax.ppermute(block, axis, route)


def on_device(front_panel, front_trail, child_panel, child_trail, child_map, child_count):
    block_rows, panel_cols = front_panel.shape
    trail_cols = front_trail.shape[1]
    slab_rows = child_map.shape[1]
    panel_width = panel_cols * lax.axis_size("col")
    top_bit = lax.axis_size("row").bit_length() - 2
    row_id = lax.axis_index("row")
    col_id = lax.axis_index("col")
    live_rows = jnp.arange(slab_rows, dtype=jnp.int32)[None, :] < child_count
    targets = jnp.where(live_rows, child_map, block_rows)

    own_panel = front_panel.at[targets[0]].add(child_panel[0], mode="drop")
    partner_top = jnp.zeros((panel_width, panel_cols), jnp.float32).at[targets[1]].add(
        child_panel[1], mode="drop"
    )
    share = jnp.where(
        row_id == 0,
        own_panel[:panel_width],
        jnp.where(row_id == 1 << top_bit, partner_top, 0.0),
    )
    diag_piece = lax.psum(share, "row")
    diag_full = lax.all_gather(diag_piece, "col", axis=0)

    partner_targets = swapped(targets[1], "row", top_bit)
    panel_slab = swapped(child_panel[1], "row", top_bit)
    panel = own_panel.at[partner_targets].add(panel_slab, mode="drop")
    sibling, _ = lax.optimization_barrier((child_trail[1], panel_slab))
    trail_slab = swapped(sibling, "row", top_bit)
    trail = front_trail.at[targets[0]].add(child_trail[0], mode="drop")

    window_rows = trail_cols * lax.axis_size("col")
    blank = jnp.zeros((window_rows, panel_cols), jnp.float32)
    window = lax.dynamic_slice_in_dim(
        jnp.concatenate([blank, panel, blank], axis=0),
        jnp.maximum(window_rows + panel_width - row_id * block_rows, 0),
        window_rows,
        0,
    ).reshape(-1, trail_cols, panel_cols)
    window = lax.all_to_all(window, "col", 0, 0)
    window, _ = lax.optimization_barrier((window, diag_piece))
    window = lax.psum(window, "row")

    panel, _ = lax.optimization_barrier((panel, diag_full))
    panel_full = lax.all_gather(panel, "col", axis=0)

    upper, inverse = cholesky(diag_full)
    trail_slab, _ = lax.optimization_barrier((trail_slab, inverse))
    trail = trail.at[partner_targets].add(trail_slab, mode="drop")
    place = jnp.stack([(row_id == 0).astype(jnp.int32), col_id.astype(jnp.int32)])
    return update(place, panel_full, inverse, window, upper, trail)


def solution(mesh):
    in_specs = (
        P("row", "col"),
        P("row", "col"),
        P(None, "row", "col"),
        P(None, "row", "col"),
        P(None, "row"),
        P(None, "row"),
    )
    out_specs = (P("row", "col"), P("row", "col"))
    return jax.shard_map(
        on_device, mesh=mesh, in_specs=in_specs, out_specs=out_specs, check_vma=False
    )
```

```python
import functools

import jax
import jax.numpy as jnp
from jax import lax
from jax.experimental import pallas as pl
from jax.experimental.pallas import tpu as pltpu
from jax.sharding import PartitionSpec as P

HIGHEST = lax.Precision.HIGHEST
TILE = 128
GROUP = 16


def dot_tn(a, b, precision=HIGHEST):
    return lax.dot_general(
        a, b, (((0,), (0,)), ((), ())), precision=precision, preferred_element_type=jnp.float32
    )


def dot_nt(a, b, precision=HIGHEST):
    return lax.dot_general(
        a, b, (((1,), (1,)), ((), ())), precision=precision, preferred_element_type=jnp.float32
    )


def dot_nn(a, b, precision=HIGHEST):
    return jnp.dot(a, b, precision=precision, preferred_element_type=jnp.float32)


def factor_tile(tile):
    row = lax.broadcasted_iota(jnp.int32, (GROUP, TILE), 0)
    lane = lax.broadcasted_iota(jnp.int32, (GROUP, TILE), 1)
    groups = TILE // GROUP
    left = [tile[GROUP * g : GROUP * (g + 1), :] for g in range(groups)]
    right = [jnp.where(lane == row + GROUP * g, 1.0, 0.0) for g in range(groups)]
    for g in range(groups):
        a, x = left[g], right[g]
        cols = [
            jnp.broadcast_to(a[:, GROUP * g + i : GROUP * g + i + 1], (GROUP, TILE))
            for i in range(GROUP)
        ]
        for i in range(GROUP):
            pivot = jnp.broadcast_to(cols[i][i : i + 1, :], (GROUP, TILE))
            scale = lax.rsqrt(pivot)
            column = cols[i] * scale
            below = jnp.where(row > i, column, 0.0)
            a_row = jnp.broadcast_to(a[i : i + 1, :], (GROUP, TILE)) * scale
            x_row = jnp.broadcast_to(x[i : i + 1, :], (GROUP, TILE)) * scale
            a = jnp.where(row == i, a_row, a - below * a_row)
            x = jnp.where(row == i, x_row, x - below * x_row)
            for k in range(i + 1, GROUP):
                cols[k] = cols[k] - below * jnp.broadcast_to(column[k : k + 1, :], (GROUP, TILE))
        a = jnp.where(lane >= row + GROUP * g, a, 0.0)
        left[g], right[g] = a, x
        if g + 1 < groups:
            change = dot_tn(a, jnp.concatenate([a, x], axis=1))
            for h in range(g + 1, groups):
                part = change[GROUP * h : GROUP * (h + 1), :]
                left[h] = left[h] - part[:, :TILE]
                right[h] = right[h] - part[:, TILE:]
    return jnp.concatenate(left, axis=0), jnp.concatenate(right, axis=0)


def eliminate(first, last, upper_ref, inverse_ref):
    size = inverse_ref.shape[0]
    count = size // TILE
    block = lax.broadcasted_iota(jnp.int32, (TILE, size), 1) // TILE

    def step(b, carry):
        at = pl.multiple_of(b * TILE, TILE)
        rows, cols = pl.ds(at, TILE), pl.ds(at, TILE)
        top, inv = factor_tile(inverse_ref[rows, cols])
        scaled = dot_nn(inv, inverse_ref[rows, :])
        upper_ref[rows, :] = jnp.where(block > b, scaled, 0.0)
        upper_ref[rows, cols] = top
        inverse_ref[rows, :] = scaled
        inverse_ref[rows, cols] = inv

        def below(s, inner):
            under = pl.ds(pl.multiple_of(s * TILE, TILE), TILE)
            change = dot_tn(upper_ref[rows, under], inverse_ref[rows, :])
            inverse_ref[under, :] = jnp.where(block == b, 0.0, inverse_ref[under, :]) - change
            return inner

        lax.fori_loop(b + 1, count, below, 0)
        inverse_ref[rows, :] = jnp.where(block <= b, inverse_ref[rows, :], 0.0)
        return carry

    lax.fori_loop(first, last, step, 0)


def first_kernel(last, diag_ref, upper_ref, inverse_ref):
    pieces, size, narrow = diag_ref.shape
    count = size // TILE
    per = TILE // narrow

    def tile(i, j):
        rows = slice(TILE * i, TILE * (i + 1))
        parts = [diag_ref[piece, rows, :] for piece in range(per * j, per * (j + 1))]
        return parts[0] if per == 1 else jnp.concatenate(parts, axis=1)

    for i in range(count):
        for j in range(i, count):
            inverse_ref[TILE * i : TILE * (i + 1), TILE * j : TILE * (j + 1)] = 0.5 * (
                tile(i, j) + tile(j, i).T
            )
        if i:
            inverse_ref[TILE * i : TILE * (i + 1), : TILE * i] = jnp.zeros(
                (TILE, TILE * i), jnp.float32
            )
    eliminate(0, last, upper_ref, inverse_ref)


def next_kernel(first, last, upper_in, inverse_in, upper_ref, inverse_ref):
    upper_ref[...] = upper_in[...]
    inverse_ref[...] = inverse_in[...]
    eliminate(first, last, upper_ref, inverse_ref)


def cholesky_part(first, last, *operands):
    size = operands[0].shape[-2]
    shape = jax.ShapeDtypeStruct((size, size), jnp.float32)
    if first:
        kernel = functools.partial(next_kernel, first, last)
    else:
        kernel = functools.partial(first_kernel, last)
    return pl.pallas_call(
        kernel,
        out_shape=(shape, shape),
        in_specs=[pl.BlockSpec(memory_space=pltpu.VMEM)] * len(operands),
        out_specs=(pl.BlockSpec(memory_space=pltpu.VMEM),) * 2,
        compiler_params=pltpu.CompilerParams(vmem_limit_bytes=40 << 20),
        cost_estimate=pl.CostEstimate(
            flops=7_500_000_000 * (last - first),
            bytes_accessed=12 * size * size,
            transcendentals=0,
        ),
        name="cholesky_and_inverse",
    )(*operands)


def halves(value):
    high = value.astype(jnp.bfloat16)
    return high, (value - high.astype(jnp.float32)).astype(jnp.bfloat16)


def dot_split(dims, left, right):
    def dot(x, y):
        return lax.dot_general(x, y, (dims, ((), ())), preferred_element_type=jnp.float32)

    return (dot(left[0], right[1]) + dot(left[1], right[0])) + dot(left[0], right[0])


def joined(ref):
    return jnp.concatenate([ref[piece] for piece in range(ref.shape[0])], axis=1)


def update_kernel(
    top_tiles, place_ref, panel_ref, inverse_ref, window_ref, upper_ref, trail_ref,
    factor_ref, schur_ref, high_ref, low_ref, flipped_ref, first_ref,
):
    step = pl.program_id(0)
    depth = inverse_ref.shape[0]
    size, width = trail_ref.shape
    narrow = upper_ref.shape[0]
    at_root = place_ref[0] == 1
    part = 256

    @pl.when(step == 0)
    def _():
        window = joined(window_ref)
        window_halves = halves(window)
        for i in range(0, depth, part):
            end = i + part
            first_ref[i:end, :] = dot_split(
                ((1,), (1,)),
                halves(inverse_ref[i:end, :end]),
                tuple(half[:, :end] for half in window_halves),
            )
        for i in range(0, depth, part):
            second = dot_split(
                ((0,), (0,)), halves(inverse_ref[i:, i : i + part]), halves(first_ref[i:, :])
            )
            high_ref[i : i + part, :width], low_ref[i : i + part, :width] = halves(second)
        own = pl.ds(pl.multiple_of(place_ref[1] * narrow, narrow), narrow)
        high_ref[:, width:], low_ref[:, width:] = halves(inverse_ref[own, :].T)

        @pl.when(at_root)
        def _():
            flipped_ref[...] = window.T

    in_top = jnp.logical_and(at_root, step < top_tiles)

    @pl.when(in_top)
    def _():
        rows = pl.ds(pl.multiple_of(step * size, size), size)
        factor_ref[...] = upper_ref[:, rows].T
        schur_ref[...] = trail_ref[...] - flipped_ref[rows, :]

    @pl.when(jnp.logical_not(in_top))
    def _():
        product = dot_split(
            ((1,), (0,)), halves(joined(panel_ref)), (high_ref[...], low_ref[...])
        )
        factor_ref[...] = product[:, width:]
        schur_ref[...] = trail_ref[...] - product[:, :width]


def update(place, panel, inverse, window, upper, trail):
    pieces, rows, narrow = panel.shape
    depth = inverse.shape[0]
    width = trail.shape[1]
    size = 512
    return pl.pallas_call(
        functools.partial(update_kernel, depth // size),
        grid_spec=pltpu.PrefetchScalarGridSpec(
            num_scalar_prefetch=1,
            grid=(rows // size,),
            in_specs=[
                pl.BlockSpec((pieces, size, narrow), lambda i, place: (0, i, 0)),
                pl.BlockSpec((depth, depth), lambda i, place: (0, 0)),
                pl.BlockSpec((pieces, width, narrow), lambda i, place: (0, 0, 0)),
                pl.BlockSpec((narrow, depth), lambda i, place: (place[1], 0)),
                pl.BlockSpec((size, width), lambda i, place: (i, 0)),
            ],
            out_specs=(
                pl.BlockSpec((size, narrow), lambda i, place: (i, 0)),
                pl.BlockSpec((size, width), lambda i, place: (i, 0)),
            ),
            scratch_shapes=[pltpu.VMEM((depth, width + narrow), jnp.bfloat16)] * 2
            + [pltpu.VMEM((depth, width), jnp.float32)] * 2,
        ),
        out_shape=(
            jax.ShapeDtypeStruct((rows, narrow), jnp.float32),
            jax.ShapeDtypeStruct((rows, width), jnp.float32),
        ),
        compiler_params=pltpu.CompilerParams(vmem_limit_bytes=56 << 20),
        name="factor_and_schur",
    )(place, panel, inverse, window, upper, trail)


def swapped(block, axis, distance):
    count = lax.axis_size(axis)
    route = []
    for low in range(count):
        high = low | 1 << distance
        if high != low and high < count:
            route += [(low, high), (high, low)]
    return lax.ppermute(block, axis, route)


def spread(level, panel_width, trail_cols, block_rows):
    rows, cols = lax.axis_size("row"), lax.axis_size("col")
    stride = rows >> level + 1
    route = []
    for col in range(cols):
        root = (panel_width + col * trail_cols) // block_rows
        for other in range(0, rows, 2 * stride):
            here = root ^ other
            route.append((here * cols + col, (here ^ stride) * cols + col))
    return route


def on_device(front_panel, front_trail, child_panel, child_trail, child_map, child_count):
    block_rows, panel_cols = front_panel.shape
    trail_cols = front_trail.shape[1]
    slab_rows = child_map.shape[1]
    panel_width = panel_cols * lax.axis_size("col")
    top_bit = lax.axis_size("row").bit_length() - 2
    row_id = lax.axis_index("row")
    col_id = lax.axis_index("col")
    live_rows = jnp.arange(slab_rows, dtype=jnp.int32)[None, :] < child_count
    targets = jnp.where(live_rows, child_map, block_rows)

    own_panel = front_panel.at[targets[0]].add(child_panel[0], mode="drop")
    partner_top = jnp.zeros((panel_width, panel_cols), jnp.float32).at[targets[1]].add(
        child_panel[1], mode="drop"
    )
    share = jnp.where(
        row_id == 0,
        own_panel[:panel_width],
        jnp.where(row_id == 1 << top_bit, partner_top, 0.0),
    )
    diag_piece = lax.psum(share, "row")

    partner_targets = swapped(targets[1], "row", top_bit)
    panel_slab = swapped(child_panel[1], "row", top_bit)
    half = slab_rows // 2
    early_slab = swapped(child_trail[1, :half], "row", top_bit)
    late_slab = swapped(child_trail[1, half:], "row", top_bit)
    panel = own_panel.at[partner_targets].add(panel_slab, mode="drop")
    diag_piece, panel, early_slab = lax.optimization_barrier((diag_piece, panel, early_slab))
    diag_full = lax.all_gather(diag_piece, "col", axis=0)
    trail = front_trail.at[targets[0]].add(child_trail[0], mode="drop")
    trail = trail.at[partner_targets[:half]].add(early_slab, mode="drop")
    trail = trail.at[partner_targets[half:]].add(late_slab, mode="drop")

    window_rows = trail_cols * lax.axis_size("col")
    blank = jnp.zeros((window_rows, panel_cols), jnp.float32)
    window = lax.dynamic_slice_in_dim(
        jnp.concatenate([blank, panel, blank], axis=0),
        jnp.maximum(window_rows + panel_width - row_id * block_rows, 0),
        window_rows,
        0,
    ).reshape(-1, trail_cols, panel_cols)
    window = lax.all_to_all(window, "col", 0, 0)

    diag_full, panel, window, trail = lax.optimization_barrier((diag_full, panel, window, trail))
    panel_full = lax.all_gather(panel, "col", axis=0)

    count = panel_width // TILE
    state = (diag_full,)
    for level in range(top_bit + 1):
        route = spread(level, panel_width, trail_cols, block_rows)
        arrived = lax.ppermute(window, ("row", "col"), route)
        first, last = (count * at // (top_bit + 1) for at in (level, level + 1))
        state = cholesky_part(first, last, *state)
        arrived, *state = lax.optimization_barrier((arrived, *state))
        window = window + arrived
        if level < top_bit:
            window, *state = lax.optimization_barrier((window, *state))
    upper, inverse = state
    place = jnp.stack([(row_id == 0).astype(jnp.int32), col_id.astype(jnp.int32)])
    return update(place, panel_full, inverse, window, upper, trail)


def solution(mesh):
    in_specs = (
        P("row", "col"),
        P("row", "col"),
        P(None, "row", "col"),
        P(None, "row", "col"),
        P(None, "row"),
        P(None, "row"),
    )
    out_specs = (P("row", "col"), P("row", "col"))
    return jax.shard_map(
        on_device, mesh=mesh, in_specs=in_specs, out_specs=out_specs, check_vma=False
    )
```

```python
import functools

import jax
import jax.numpy as jnp
from jax import lax
from jax.experimental import pallas as pl
from jax.experimental.pallas import tpu as pltpu
from jax.sharding import PartitionSpec as P

HIGHEST = lax.Precision.HIGHEST
TILE = 128
GROUP = 16


def dot_tn(a, b, precision=HIGHEST):
    return lax.dot_general(
        a, b, (((0,), (0,)), ((), ())), precision=precision, preferred_element_type=jnp.float32
    )


def dot_nt(a, b, precision=HIGHEST):
    return lax.dot_general(
        a, b, (((1,), (1,)), ((), ())), precision=precision, preferred_element_type=jnp.float32
    )


def dot_nn(a, b, precision=HIGHEST):
    return jnp.dot(a, b, precision=precision, preferred_element_type=jnp.float32)


def factor_tile(tile):
    row = lax.broadcasted_iota(jnp.int32, (GROUP, TILE), 0)
    lane = lax.broadcasted_iota(jnp.int32, (GROUP, TILE), 1)
    groups = TILE // GROUP
    left = [tile[GROUP * g : GROUP * (g + 1), :] for g in range(groups)]
    right = [jnp.where(lane == row + GROUP * g, 1.0, 0.0) for g in range(groups)]
    for g in range(groups):
        a, x = left[g], right[g]
        cols = [
            jnp.broadcast_to(a[:, GROUP * g + i : GROUP * g + i + 1], (GROUP, TILE))
            for i in range(GROUP)
        ]
        for i in range(GROUP):
            pivot = jnp.broadcast_to(cols[i][i : i + 1, :], (GROUP, TILE))
            scale = lax.rsqrt(pivot)
            column = cols[i] * scale
            below = jnp.where(row > i, column, 0.0)
            a_row = jnp.broadcast_to(a[i : i + 1, :], (GROUP, TILE)) * scale
            x_row = jnp.broadcast_to(x[i : i + 1, :], (GROUP, TILE)) * scale
            a = jnp.where(row == i, a_row, a - below * a_row)
            x = jnp.where(row == i, x_row, x - below * x_row)
            for k in range(i + 1, GROUP):
                cols[k] = cols[k] - below * jnp.broadcast_to(column[k : k + 1, :], (GROUP, TILE))
        a = jnp.where(lane >= row + GROUP * g, a, 0.0)
        left[g], right[g] = a, x
        if g + 1 < groups:
            change = dot_tn(a, jnp.concatenate([a, x], axis=1))
            for h in range(g + 1, groups):
                part = change[GROUP * h : GROUP * (h + 1), :]
                left[h] = left[h] - part[:, :TILE]
                right[h] = right[h] - part[:, TILE:]
    return jnp.concatenate(left, axis=0), jnp.concatenate(right, axis=0)


def eliminate(first, last, upper_ref, inverse_ref):
    size = inverse_ref.shape[0]
    count = size // TILE
    block = lax.broadcasted_iota(jnp.int32, (TILE, size), 1) // TILE

    def step(b, carry):
        at = pl.multiple_of(b * TILE, TILE)
        rows, cols = pl.ds(at, TILE), pl.ds(at, TILE)
        top, inv = factor_tile(inverse_ref[rows, cols])
        scaled = dot_nn(inv, inverse_ref[rows, :])
        upper_ref[rows, :] = jnp.where(block > b, scaled, 0.0)
        upper_ref[rows, cols] = top
        inverse_ref[rows, :] = scaled
        inverse_ref[rows, cols] = inv

        def below(s, inner):
            under = pl.ds(pl.multiple_of(s * TILE, TILE), TILE)
            change = dot_tn(upper_ref[rows, under], inverse_ref[rows, :])
            inverse_ref[under, :] = jnp.where(block == b, 0.0, inverse_ref[under, :]) - change
            return inner

        lax.fori_loop(b + 1, count, below, 0)
        inverse_ref[rows, :] = jnp.where(block <= b, inverse_ref[rows, :], 0.0)
        return carry

    lax.fori_loop(first, last, step, 0)


def first_kernel(last, diag_ref, upper_ref, inverse_ref):
    pieces, size, narrow = diag_ref.shape
    count = size // TILE
    per = TILE // narrow

    def tile(i, j):
        rows = slice(TILE * i, TILE * (i + 1))
        parts = [diag_ref[piece, rows, :] for piece in range(per * j, per * (j + 1))]
        return parts[0] if per == 1 else jnp.concatenate(parts, axis=1)

    for i in range(count):
        for j in range(i, count):
            inverse_ref[TILE * i : TILE * (i + 1), TILE * j : TILE * (j + 1)] = 0.5 * (
                tile(i, j) + tile(j, i).T
            )
        if i:
            inverse_ref[TILE * i : TILE * (i + 1), : TILE * i] = jnp.zeros(
                (TILE, TILE * i), jnp.float32
            )
    eliminate(0, last, upper_ref, inverse_ref)


def next_kernel(first, last, upper_in, inverse_in, upper_ref, inverse_ref):
    upper_ref[...] = upper_in[...]
    inverse_ref[...] = inverse_in[...]
    eliminate(first, last, upper_ref, inverse_ref)


def cholesky_part(first, last, *operands):
    size = operands[0].shape[-2]
    shape = jax.ShapeDtypeStruct((size, size), jnp.float32)
    if first:
        kernel = functools.partial(next_kernel, first, last)
    else:
        kernel = functools.partial(first_kernel, last)
    return pl.pallas_call(
        kernel,
        out_shape=(shape, shape),
        in_specs=[pl.BlockSpec(memory_space=pltpu.VMEM)] * len(operands),
        out_specs=(pl.BlockSpec(memory_space=pltpu.VMEM),) * 2,
        compiler_params=pltpu.CompilerParams(vmem_limit_bytes=40 << 20),
        cost_estimate=pl.CostEstimate(
            flops=7_500_000_000 * (last - first),
            bytes_accessed=12 * size * size,
            transcendentals=0,
        ),
        name="cholesky_and_inverse",
    )(*operands)


def halves(value):
    high = value.astype(jnp.bfloat16)
    return high, (value - high.astype(jnp.float32)).astype(jnp.bfloat16)


def dot_split(dims, left, right):
    def dot(x, y):
        return lax.dot_general(x, y, (dims, ((), ())), preferred_element_type=jnp.float32)

    return (dot(left[0], right[1]) + dot(left[1], right[0])) + dot(left[0], right[0])


def joined(ref):
    return jnp.concatenate([ref[piece] for piece in range(ref.shape[0])], axis=1)


def update_kernel(
    top_tiles, place_ref, panel_ref, inverse_ref, window_ref, upper_ref, trail_ref,
    factor_ref, schur_ref, high_ref, low_ref, flipped_ref, first_ref,
):
    step = pl.program_id(0)
    depth = inverse_ref.shape[0]
    size, width = trail_ref.shape
    narrow = upper_ref.shape[0]
    at_root = place_ref[0] == 1
    part = 256

    @pl.when(step == 0)
    def _():
        window = joined(window_ref)
        window_halves = halves(window)
        for i in range(0, depth, part):
            end = i + part
            first_ref[i:end, :] = dot_split(
                ((1,), (1,)),
                halves(inverse_ref[i:end, :end]),
                tuple(half[:, :end] for half in window_halves),
            )
        for i in range(0, depth, part):
            second = dot_split(
                ((0,), (0,)), halves(inverse_ref[i:, i : i + part]), halves(first_ref[i:, :])
            )
            high_ref[i : i + part, :width], low_ref[i : i + part, :width] = halves(second)
        own = pl.ds(pl.multiple_of(place_ref[1] * narrow, narrow), narrow)
        high_ref[:, width:], low_ref[:, width:] = halves(inverse_ref[own, :].T)

        @pl.when(at_root)
        def _():
            flipped_ref[...] = window.T

    in_top = jnp.logical_and(at_root, step < top_tiles)

    @pl.when(in_top)
    def _():
        rows = pl.ds(pl.multiple_of(step * size, size), size)
        factor_ref[...] = upper_ref[:, rows].T
        schur_ref[...] = trail_ref[...] - flipped_ref[rows, :]

    @pl.when(jnp.logical_not(in_top))
    def _():
        product = dot_split(
            ((1,), (0,)), halves(joined(panel_ref)), (high_ref[...], low_ref[...])
        )
        factor_ref[...] = product[:, width:]
        schur_ref[...] = trail_ref[...] - product[:, :width]


def update(place, panel, inverse, window, upper, trail):
    pieces, rows, narrow = panel.shape
    depth = inverse.shape[0]
    width = trail.shape[1]
    size = 512
    return pl.pallas_call(
        functools.partial(update_kernel, depth // size),
        grid_spec=pltpu.PrefetchScalarGridSpec(
            num_scalar_prefetch=1,
            grid=(rows // size,),
            in_specs=[
                pl.BlockSpec((pieces, size, narrow), lambda i, place: (0, i, 0)),
                pl.BlockSpec((depth, depth), lambda i, place: (0, 0)),
                pl.BlockSpec((pieces, width, narrow), lambda i, place: (0, 0, 0)),
                pl.BlockSpec((narrow, depth), lambda i, place: (place[1], 0)),
                pl.BlockSpec((size, width), lambda i, place: (i, 0)),
            ],
            out_specs=(
                pl.BlockSpec((size, narrow), lambda i, place: (i, 0)),
                pl.BlockSpec((size, width), lambda i, place: (i, 0)),
            ),
            scratch_shapes=[pltpu.VMEM((depth, width + narrow), jnp.bfloat16)] * 2
            + [pltpu.VMEM((depth, width), jnp.float32)] * 2,
        ),
        out_shape=(
            jax.ShapeDtypeStruct((rows, narrow), jnp.float32),
            jax.ShapeDtypeStruct((rows, width), jnp.float32),
        ),
        compiler_params=pltpu.CompilerParams(vmem_limit_bytes=56 << 20),
        name="factor_and_schur",
    )(place, panel, inverse, window, upper, trail)


def swapped(block, axis, distance):
    count = lax.axis_size(axis)
    route = []
    for low in range(count):
        high = low | 1 << distance
        if high != low and high < count:
            route += [(low, high), (high, low)]
    return lax.ppermute(block, axis, route)


def spread(level, panel_width, trail_cols, block_rows):
    rows, cols = lax.axis_size("row"), lax.axis_size("col")
    stride = rows >> level + 1
    route = []
    for col in range(cols):
        root = (panel_width + col * trail_cols) // block_rows
        for other in range(0, rows, 2 * stride):
            here = root ^ other
            route.append((here * cols + col, (here ^ stride) * cols + col))
    return route


def on_device(front_panel, front_trail, child_panel, child_trail, child_map, child_count):
    block_rows, panel_cols = front_panel.shape
    trail_cols = front_trail.shape[1]
    slab_rows = child_map.shape[1]
    panel_width = panel_cols * lax.axis_size("col")
    top_bit = lax.axis_size("row").bit_length() - 2
    row_id = lax.axis_index("row")
    col_id = lax.axis_index("col")
    live_rows = jnp.arange(slab_rows, dtype=jnp.int32)[None, :] < child_count
    targets = jnp.where(live_rows, child_map, block_rows)

    is_root, is_partner = row_id == 0, row_id == 1 << top_bit
    share = jnp.where(is_root, front_panel[:panel_width], 0.0)
    share = share.at[jnp.where(is_partner, targets[1], targets[0])].add(
        jnp.where(is_partner, child_panel[1], jnp.where(is_root, child_panel[0], 0.0)),
        mode="drop",
    )
    diag_piece = lax.psum(share, "row")

    partner_targets = swapped(targets[1], "row", top_bit)
    panel_slab = swapped(child_panel[1], "row", top_bit)
    half = slab_rows // 2
    early_slab = swapped(child_trail[1, :half], "row", top_bit)
    panel = front_panel.at[targets[0]].add(child_panel[0], mode="drop")
    panel = panel.at[partner_targets].add(panel_slab, mode="drop")
    diag_piece, panel, front_trail = lax.optimization_barrier((diag_piece, panel, front_trail))
    diag_full = lax.all_gather(diag_piece, "col", axis=0)
    trail = front_trail.at[targets[0]].add(child_trail[0], mode="drop")
    trail = trail.at[partner_targets[:half]].add(early_slab, mode="drop")

    window_rows = trail_cols * lax.axis_size("col")
    blank = jnp.zeros((window_rows, panel_cols), jnp.float32)
    window = lax.dynamic_slice_in_dim(
        jnp.concatenate([blank, panel, blank], axis=0),
        jnp.maximum(window_rows + panel_width - row_id * block_rows, 0),
        window_rows,
        0,
    ).reshape(-1, trail_cols, panel_cols)
    window = lax.all_to_all(window, "col", 0, 0)

    diag_full, panel, window, trail = lax.optimization_barrier((diag_full, panel, window, trail))
    panel_full = lax.all_gather(panel, "col", axis=0)

    count = panel_width // TILE
    state = (diag_full,)
    for level in range(top_bit + 1):
        route = spread(level, panel_width, trail_cols, block_rows)
        arrived = lax.ppermute(window, ("row", "col"), route)
        first, last = (count * at // (top_bit + 1) for at in (level, level + 1))
        state = cholesky_part(first, last, *state)
        arrived, *state = lax.optimization_barrier((arrived, *state))
        window = window + arrived
        if level < top_bit:
            window, *state = lax.optimization_barrier((window, *state))
        if level == top_bit - 1:
            late_slab, _ = lax.optimization_barrier((child_trail[1, half:], arrived))
            late_slab = swapped(late_slab, "row", top_bit)
    upper, inverse = state
    late_slab, inverse, panel_full = lax.optimization_barrier((late_slab, inverse, panel_full))
    trail = trail.at[partner_targets[half:]].add(late_slab, mode="drop")
    place = jnp.stack([(row_id == 0).astype(jnp.int32), col_id.astype(jnp.int32)])
    return update(place, panel_full, inverse, window, upper, trail)


def solution(mesh):
    in_specs = (
        P("row", "col"),
        P("row", "col"),
        P(None, "row", "col"),
        P(None, "row", "col"),
        P(None, "row"),
        P(None, "row"),
    )
    out_specs = (P("row", "col"), P("row", "col"))
    return jax.shard_map(
        on_device, mesh=mesh, in_specs=in_specs, out_specs=out_specs, check_vma=False
    )
```

```python
import functools

import jax
import jax.numpy as jnp
from jax import lax
from jax.experimental import pallas as pl
from jax.experimental.pallas import tpu as pltpu
from jax.sharding import PartitionSpec as P

HIGHEST = lax.Precision.HIGHEST
TILE = 128
GROUP = 16


def dot_tn(a, b, precision=HIGHEST):
    return lax.dot_general(
        a, b, (((0,), (0,)), ((), ())), precision=precision, preferred_element_type=jnp.float32
    )


def dot_nt(a, b, precision=HIGHEST):
    return lax.dot_general(
        a, b, (((1,), (1,)), ((), ())), precision=precision, preferred_element_type=jnp.float32
    )


def dot_nn(a, b, precision=HIGHEST):
    return jnp.dot(a, b, precision=precision, preferred_element_type=jnp.float32)


def factor_tile(tile):
    row = lax.broadcasted_iota(jnp.int32, (GROUP, TILE), 0)
    lane = lax.broadcasted_iota(jnp.int32, (GROUP, TILE), 1)
    groups = TILE // GROUP
    left = [tile[GROUP * g : GROUP * (g + 1), :] for g in range(groups)]
    right = [jnp.where(lane == row + GROUP * g, 1.0, 0.0) for g in range(groups)]
    for g in range(groups):
        a, x = left[g], right[g]
        cols = [
            jnp.broadcast_to(a[:, GROUP * g + i : GROUP * g + i + 1], (GROUP, TILE))
            for i in range(GROUP)
        ]
        for i in range(GROUP):
            pivot = jnp.broadcast_to(cols[i][i : i + 1, :], (GROUP, TILE))
            scale = lax.rsqrt(pivot)
            column = cols[i] * scale
            below = jnp.where(row > i, column, 0.0)
            a_row = jnp.broadcast_to(a[i : i + 1, :], (GROUP, TILE)) * scale
            x_row = jnp.broadcast_to(x[i : i + 1, :], (GROUP, TILE)) * scale
            a = jnp.where(row == i, a_row, a - below * a_row)
            x = jnp.where(row == i, x_row, x - below * x_row)
            for k in range(i + 1, GROUP):
                cols[k] = cols[k] - below * jnp.broadcast_to(column[k : k + 1, :], (GROUP, TILE))
        a = jnp.where(lane >= row + GROUP * g, a, 0.0)
        left[g], right[g] = a, x
        if g + 1 < groups:
            change = dot_tn(a, jnp.concatenate([a, x], axis=1))
            for h in range(g + 1, groups):
                part = change[GROUP * h : GROUP * (h + 1), :]
                left[h] = left[h] - part[:, :TILE]
                right[h] = right[h] - part[:, TILE:]
    return jnp.concatenate(left, axis=0), jnp.concatenate(right, axis=0)


def eliminate(first, last, upper_ref, inverse_ref):
    size = inverse_ref.shape[0]
    count = size // TILE
    block = lax.broadcasted_iota(jnp.int32, (TILE, size), 1) // TILE

    def step(b, carry):
        at = pl.multiple_of(b * TILE, TILE)
        rows, cols = pl.ds(at, TILE), pl.ds(at, TILE)
        top, inv = factor_tile(inverse_ref[rows, cols])
        scaled = dot_nn(inv, inverse_ref[rows, :])
        upper_ref[rows, :] = jnp.where(block > b, scaled, 0.0)
        upper_ref[rows, cols] = top
        inverse_ref[rows, :] = scaled
        inverse_ref[rows, cols] = inv

        def below(s, inner):
            under = pl.ds(pl.multiple_of(s * TILE, TILE), TILE)
            change = dot_tn(upper_ref[rows, under], inverse_ref[rows, :])
            inverse_ref[under, :] = jnp.where(block == b, 0.0, inverse_ref[under, :]) - change
            return inner

        lax.fori_loop(b + 1, count, below, 0)
        inverse_ref[rows, :] = jnp.where(block <= b, inverse_ref[rows, :], 0.0)
        return carry

    lax.fori_loop(first, last, step, 0)


def first_kernel(last, diag_ref, upper_ref, inverse_ref):
    pieces, size, narrow = diag_ref.shape
    count = size // TILE
    per = TILE // narrow

    def tile(i, j):
        rows = slice(TILE * i, TILE * (i + 1))
        parts = [diag_ref[piece, rows, :] for piece in range(per * j, per * (j + 1))]
        return parts[0] if per == 1 else jnp.concatenate(parts, axis=1)

    for i in range(count):
        for j in range(i, count):
            inverse_ref[TILE * i : TILE * (i + 1), TILE * j : TILE * (j + 1)] = 0.5 * (
                tile(i, j) + tile(j, i).T
            )
        if i:
            inverse_ref[TILE * i : TILE * (i + 1), : TILE * i] = jnp.zeros(
                (TILE, TILE * i), jnp.float32
            )
    eliminate(0, last, upper_ref, inverse_ref)


def next_kernel(first, last, upper_in, inverse_in, upper_ref, inverse_ref):
    upper_ref[...] = upper_in[...]
    inverse_ref[...] = inverse_in[...]
    eliminate(first, last, upper_ref, inverse_ref)


def cholesky_part(first, last, *operands):
    size = operands[0].shape[-2]
    shape = jax.ShapeDtypeStruct((size, size), jnp.float32)
    if first:
        kernel = functools.partial(next_kernel, first, last)
    else:
        kernel = functools.partial(first_kernel, last)
    return pl.pallas_call(
        kernel,
        out_shape=(shape, shape),
        in_specs=[pl.BlockSpec(memory_space=pltpu.VMEM)] * len(operands),
        out_specs=(pl.BlockSpec(memory_space=pltpu.VMEM),) * 2,
        compiler_params=pltpu.CompilerParams(vmem_limit_bytes=40 << 20),
        cost_estimate=pl.CostEstimate(
            flops=7_500_000_000 * (last - first),
            bytes_accessed=12 * size * size,
            transcendentals=0,
        ),
        name="cholesky_and_inverse",
    )(*operands)


def halves(value):
    high = value.astype(jnp.bfloat16)
    return high, (value - high.astype(jnp.float32)).astype(jnp.bfloat16)


def dot_split(dims, left, right):
    def dot(x, y):
        return lax.dot_general(x, y, (dims, ((), ())), preferred_element_type=jnp.float32)

    return (dot(left[0], right[1]) + dot(left[1], right[0])) + dot(left[0], right[0])


def joined(ref):
    return jnp.concatenate([ref[piece] for piece in range(ref.shape[0])], axis=1)


def update_kernel(
    top_tiles, place_ref, panel_ref, inverse_ref, window_ref, upper_ref, trail_ref,
    factor_ref, schur_ref, high_ref, low_ref, flipped_ref, first_ref,
):
    step = pl.program_id(0)
    depth = inverse_ref.shape[0]
    size, width = trail_ref.shape
    narrow = upper_ref.shape[0]
    at_root = place_ref[0] == 1
    part = 256

    @pl.when(step == 0)
    def _():
        window = joined(window_ref)
        window_halves = halves(window)
        for i in range(0, depth, part):
            end = i + part
            first_ref[i:end, :] = dot_split(
                ((1,), (1,)),
                halves(inverse_ref[i:end, :end]),
                tuple(half[:, :end] for half in window_halves),
            )
        for i in range(0, depth, part):
            second = dot_split(
                ((0,), (0,)), halves(inverse_ref[i:, i : i + part]), halves(first_ref[i:, :])
            )
            high_ref[i : i + part, :width], low_ref[i : i + part, :width] = halves(second)
        own = pl.ds(pl.multiple_of(place_ref[1] * narrow, narrow), narrow)
        high_ref[:, width:], low_ref[:, width:] = halves(inverse_ref[own, :].T)

        @pl.when(at_root)
        def _():
            flipped_ref[...] = window.T

    in_top = jnp.logical_and(at_root, step < top_tiles)

    @pl.when(in_top)
    def _():
        rows = pl.ds(pl.multiple_of(step * size, size), size)
        factor_ref[...] = upper_ref[:, rows].T
        schur_ref[...] = trail_ref[...] - flipped_ref[rows, :]

    @pl.when(jnp.logical_not(in_top))
    def _():
        product = dot_split(
            ((1,), (0,)), halves(joined(panel_ref)), (high_ref[...], low_ref[...])
        )
        factor_ref[...] = product[:, width:]
        schur_ref[...] = trail_ref[...] - product[:, :width]


def update(place, panel, inverse, window, upper, trail):
    pieces, rows, narrow = panel.shape
    depth = inverse.shape[0]
    width = trail.shape[1]
    size = 512
    return pl.pallas_call(
        functools.partial(update_kernel, depth // size),
        grid_spec=pltpu.PrefetchScalarGridSpec(
            num_scalar_prefetch=1,
            grid=(rows // size,),
            in_specs=[
                pl.BlockSpec((pieces, size, narrow), lambda i, place: (0, i, 0)),
                pl.BlockSpec((depth, depth), lambda i, place: (0, 0)),
                pl.BlockSpec((pieces, width, narrow), lambda i, place: (0, 0, 0)),
                pl.BlockSpec((narrow, depth), lambda i, place: (place[1], 0)),
                pl.BlockSpec((size, width), lambda i, place: (i, 0)),
            ],
            out_specs=(
                pl.BlockSpec((size, narrow), lambda i, place: (i, 0)),
                pl.BlockSpec((size, width), lambda i, place: (i, 0)),
            ),
            scratch_shapes=[pltpu.VMEM((depth, width + narrow), jnp.bfloat16)] * 2
            + [pltpu.VMEM((depth, width), jnp.float32)] * 2,
        ),
        out_shape=(
            jax.ShapeDtypeStruct((rows, narrow), jnp.float32),
            jax.ShapeDtypeStruct((rows, width), jnp.float32),
        ),
        compiler_params=pltpu.CompilerParams(vmem_limit_bytes=56 << 20),
        cost_estimate=pl.CostEstimate(
            flops=6 * rows * depth * (width + narrow) + 12 * depth * depth * width,
            bytes_accessed=4 * rows * (depth + 2 * (width + narrow)),
            transcendentals=0,
        ),
        name="factor_and_schur",
    )(place, panel, inverse, window, upper, trail)


def swapped(block, axis, distance):
    count = lax.axis_size(axis)
    route = []
    for low in range(count):
        high = low | 1 << distance
        if high != low and high < count:
            route += [(low, high), (high, low)]
    return lax.ppermute(block, axis, route)


def spread(level, panel_width, trail_cols, block_rows):
    rows, cols = lax.axis_size("row"), lax.axis_size("col")
    stride = rows >> level + 1
    route = []
    for col in range(cols):
        root = (panel_width + col * trail_cols) // block_rows
        for other in range(0, rows, 2 * stride):
            here = root ^ other
            route.append((here * cols + col, (here ^ stride) * cols + col))
    return route


def on_device(front_panel, front_trail, child_panel, child_trail, child_map, child_count):
    block_rows, panel_cols = front_panel.shape
    trail_cols = front_trail.shape[1]
    slab_rows = child_map.shape[1]
    panel_width = panel_cols * lax.axis_size("col")
    top_bit = lax.axis_size("row").bit_length() - 2
    row_id = lax.axis_index("row")
    col_id = lax.axis_index("col")
    live_rows = jnp.arange(slab_rows, dtype=jnp.int32)[None, :] < child_count
    targets = jnp.where(live_rows, child_map, block_rows)

    is_root, is_partner = row_id == 0, row_id == 1 << top_bit
    share = jnp.where(is_root, front_panel[:panel_width], 0.0)
    share = share.at[jnp.where(is_partner, targets[1], targets[0])].add(
        jnp.where(is_partner, child_panel[1], jnp.where(is_root, child_panel[0], 0.0)),
        mode="drop",
    )
    diag_piece = lax.psum(share, "row")

    partner_targets = swapped(targets[1], "row", top_bit)
    panel_slab = swapped(child_panel[1], "row", top_bit)
    half = slab_rows // 2
    early_slab = swapped(child_trail[1, :half], "row", top_bit)
    panel = front_panel.at[targets[0]].add(child_panel[0], mode="drop")
    panel = panel.at[partner_targets].add(panel_slab, mode="drop")
    diag_piece, panel, front_trail = lax.optimization_barrier((diag_piece, panel, front_trail))
    diag_full = lax.all_gather(diag_piece, "col", axis=0)
    trail = front_trail.at[targets[0]].add(child_trail[0], mode="drop")
    trail = trail.at[partner_targets[:half]].add(early_slab, mode="drop")

    window_rows = trail_cols * lax.axis_size("col")
    blank = jnp.zeros((window_rows, panel_cols), jnp.float32)
    window = lax.dynamic_slice_in_dim(
        jnp.concatenate([blank, panel, blank], axis=0),
        jnp.maximum(window_rows + panel_width - row_id * block_rows, 0),
        window_rows,
        0,
    ).reshape(-1, trail_cols, panel_cols)
    window = lax.all_to_all(window, "col", 0, 0)

    diag_full, panel, window, trail = lax.optimization_barrier((diag_full, panel, window, trail))
    panel_full = lax.all_gather(panel, "col", axis=0)

    count = panel_width // TILE
    state = (diag_full,)
    for level in range(top_bit + 1):
        route = spread(level, panel_width, trail_cols, block_rows)
        arrived = lax.ppermute(window, ("row", "col"), route)
        first, last = (count * at // (top_bit + 1) for at in (level, level + 1))
        state = cholesky_part(first, last, *state)
        arrived, *state = lax.optimization_barrier((arrived, *state))
        window = window + arrived
        if level < top_bit:
            window, *state = lax.optimization_barrier((window, *state))
    panel_full, window = lax.optimization_barrier((panel_full, window))
    upper, inverse = state

    late_slab, window = lax.optimization_barrier((child_trail[1, half:], window))
    late_slab = swapped(late_slab, "row", top_bit)
    place = jnp.stack([(row_id == 0).astype(jnp.int32), col_id.astype(jnp.int32)])
    factor_block, schur_block = update(place, panel_full, inverse, window, upper, trail)
    late_slab, schur_block = lax.optimization_barrier((late_slab, schur_block))
    schur_block = schur_block.at[partner_targets[half:]].add(late_slab, mode="drop")
    return factor_block, schur_block


def solution(mesh):
    in_specs = (
        P("row", "col"),
        P("row", "col"),
        P(None, "row", "col"),
        P(None, "row", "col"),
        P(None, "row"),
        P(None, "row"),
    )
    out_specs = (P("row", "col"), P("row", "col"))
    return jax.shard_map(
        on_device, mesh=mesh, in_specs=in_specs, out_specs=out_specs, check_vma=False
    )
```
